32 devices in a mesh: mol: 2 (over y), amp: 4 (over z), summa: 2 (over x), rep: 2 (over core).
Axes of the slice: x: 2, y: 2, z: 4, core: 2. Of those that a mesh axis runs over, the one named last changes fastest.
Arguments:
- integrals: float32 [200, 512, 4, 100], P(('mol', 'summa'), ('amp', 'rep')), parts along dimension 0, may hold values from -0.078125 to 0.078125
- amplitudes: float32 [200, 64, 512, 100], P(('mol', 'summa'), ('amp', 'rep')), parts along dimension 0, may hold values from -6 to 6
- occ_irreps: int32 [200], P('mol'), parts along dimension 0, may hold values from 0 to 7
- virt_irreps: int32 [16], P('mol'), parts along dimension 0, may hold values from 0 to 7
Outputs:
- cycle: float32 [8, 100, 64, 100], P(('mol', 'summa'), None, ('amp', 'rep')), parts along dimension 0
The draws below stay inside these ranges and needn't reach their ends.
There are 2 independent parts, one for each index of `mol`. The reference program is written for one: setup_inputs(seed, part) draws one part's arguments, and reference() takes and returns one part's arrays. A program takes and returns all parts, laid end to end along the dimension named above; each array names one. Nothing has to cross between parts.
All inputs are finite; a program needn't handle non-finite values.
Results may differ from the reference program's by a relative error of at most 0.00007.
Values sent between devices are 32-bit elements; how exact they have to be, the bound alone decides.
No kernel may reach another device: no remote copies, remote signals or barrier semaphores. Data moves between devices by JAX's collectives and lax.ppermute only.
A program may use at most 384 MiB of HBM per device.

```python
import jax
import jax.numpy as jnp
from jax import lax

O = 100
V = 512
TILE = 64
A = 4
B = 64
NVT = 8


def plant(values, stream_key, smallest, high):
    dims = values.shape
    place = [jax.random.randint(jax.random.fold_in(stream_key, axis), (), 0, dims[axis]) for axis in range(len(dims))]
    values = values.at[tuple(place)].set(smallest)
    longest = dims.index(max(dims))
    place[longest] = (place[longest] + 1) % dims[longest]
    return values.at[tuple(place)].set(high)


def level_of(rng, shape, split, low, high):
    loudness, own = 1.0, jax.random.fold_in(rng, 6)
    for position, blocks in split:
        steps = jnp.exp(jax.random.uniform(jax.random.fold_in(own, position), (blocks,), jnp.float32, low / len(split), high / len(split)))
        loudness = loudness * jnp.repeat(steps, shape[position] // blocks).reshape([-1 if axis == position else 1 for axis in range(len(shape))])
    return loudness


def centred(stream_key, dims, deviation, limit, pieces=(), held_as=jnp.bfloat16):
    result = jax.random.normal(stream_key, dims, jnp.float32) * deviation
    if len(pieces) > 0:
        result = level_of(stream_key, dims, pieces, -0.22, 0.18) * result
    return jnp.clip(result, min=-limit, max=limit).astype(held_as)


def setup_inputs(seed: int = 0, part: int = 0) -> dict:
    key_list = jax.random.split(jax.random.key(seed), 5)
    part_keys = jax.random.split(jax.random.fold_in(key_list[4], part), 5)
    return {
        "integrals": centred(part_keys[0], (O, V, A, O), (O * V // 8) ** -0.5, 0.078125, ((0, 2), (1, 8)), jnp.float32),
        "amplitudes": centred(part_keys[1], (O, B, V, O), 1.0, 6.0, ((0, 2), (1, 8)), jnp.float32),
        "occ_irreps": plant(jax.random.randint(part_keys[2], (O,), 0, 8), jax.random.fold_in(part_keys[2], 1), 0, 7).astype(jnp.int32),
        "virt_irreps": plant(jax.random.randint(part_keys[3], (NVT,), 0, 8), jax.random.fold_in(part_keys[3], 1), 0, 7).astype(jnp.int32),
    }


def reference(integrals, amplitudes, occ_irreps, virt_irreps):
    tile_ids = jnp.arange(V, dtype=jnp.int32) // TILE
    virt_labels = virt_irreps[tile_ids]
    allowed = (occ_irreps[:, None] == virt_labels[None, :]).astype(jnp.float32)
    masked = integrals * allowed[:, :, None, None]
    return jnp.einsum("kcai,kbcj->aibj", masked, amplitudes, precision=lax.Precision.HIGHEST, preferred_element_type=jnp.float32)
```

```python
import functools

import jax
import jax.numpy as jnp
from jax import lax
from jax.experimental import pallas as pl
from jax.experimental.pallas import tpu as pltpu
from jax.sharding import PartitionSpec as P

CAP = 12
DEPTH = 4
LANES = 128
VMEM_LIMIT = 40 * 1024 * 1024


def round_up(value, unit):
    return -(-value // unit) * unit


def pack_kernel(groups, ent_ref, me_ref, src_ref, out_ref, buf, sems):
    slots, c_blk, rows_a, inner = buf.shape
    blocks = src_ref.shape[1] // c_blk
    per_group = rows_a // groups
    me = me_ref[0]

    def copy(slot):
        ent = ent_ref[slot]
        return pltpu.make_async_copy(
            src_ref.at[ent // blocks, pl.ds(pl.multiple_of((ent % blocks) * c_blk, c_blk), c_blk)],
            buf.at[slot],
            sems.at[slot],
        )

    @pl.loop(0, slots)
    def _(slot):
        @pl.when(ent_ref[slot] >= 0)
        def _():
            copy(slot).start()

    @pl.loop(0, slots)
    def _(slot):
        @pl.when(ent_ref[slot] >= 0)
        def _():
            copy(slot).wait()
            for a in range(rows_a):
                phase = lax.rem(a // per_group - me + groups, groups)
                lane = (a % per_group) * c_blk
                out_ref[phase, slot, :inner, lane : lane + c_blk] = buf[slot, :, a, :].T


def pack(integrals, ent, me, groups, c_blk):
    _, _, rows_a, inner = integrals.shape
    slots = ent.shape[0]
    smem = pl.BlockSpec(memory_space=pltpu.SMEM)
    return pl.pallas_call(
        functools.partial(pack_kernel, groups),
        out_shape=jax.ShapeDtypeStruct(
            (groups, slots, round_up(inner, 8), rows_a // groups * c_blk), jnp.float32
        ),
        in_specs=[smem, smem, pl.BlockSpec(memory_space=pl.ANY)],
        out_specs=pl.BlockSpec(memory_space=pltpu.VMEM),
        scratch_shapes=[
            pltpu.VMEM((slots, c_blk, rows_a, inner), jnp.float32),
            pltpu.SemaphoreType.DMA((slots,)),
        ],
        compiler_params=pltpu.CompilerParams(vmem_limit_bytes=VMEM_LIMIT),
        name="pack_pairs",
    )(ent, me, integrals)


def contract_kernel(views, final, c_blk, n_acc, ent_ref, off_ref, *refs):
    n_src = len(views)
    srcs, amp_ref, adds, out_ref = refs[:n_src], refs[n_src], refs[n_src + 1 : n_src + 1 + n_acc], refs[n_src + 1 + n_acc]
    wall, tbuf, rhs, todo, wsem, tsem, *rest = refs[n_src + 2 + n_acc :]
    acc = rest[0] if final else out_ref
    slots, inner = wall.shape[:2]
    _, cols_j, cols_b, window = tbuf.shape
    per_group = acc.shape[2] // LANES

    copies = []
    base = 0
    for i, (ref, lead) in enumerate(zip(srcs, views)):
        view = ref.at[lead] if lead else ref
        count = ref.shape[len(lead)]
        copies.append(pltpu.make_async_copy(view, wall.at[pl.ds(base, count)], wsem.at[i]))
        copies[-1].start()
        base += count

    def note(slot, found):
        @pl.when(ent_ref[slot] >= 0)
        def _():
            todo[found] = slot

        return found + (ent_ref[slot] >= 0).astype(jnp.int32)

    total = lax.fori_loop(0, slots, note, jnp.int32(0))

    def fetch(i):
        slot = todo[i]
        place = lax.rem(i, DEPTH)
        first = pl.multiple_of((off_ref[slot] // window) * window, window)
        return pltpu.make_async_copy(
            amp_ref.at[ent_ref[slot], :, :, pl.ds(first, window)], tbuf.at[place], tsem.at[place]
        )

    for i in range(DEPTH - 1):

        @pl.when(i < total)
        def _():
            fetch(i).start()

    rhs[...] = jnp.zeros_like(rhs)
    if n_acc:
        value = adds[0][...]
        for one in adds[1:]:
            value += one[...]
        acc[...] = value
    else:
        acc[...] = jnp.zeros_like(acc)
    for one in copies:
        one.wait()

    @pl.loop(0, total)
    def _(i):
        @pl.when(i + DEPTH - 1 < total)
        def _():
            fetch(i + DEPTH - 1).start()

        slot = todo[i]
        w = wall[slot].T
        w_high = w.astype(jnp.bfloat16)
        w_low = (w - w_high.astype(jnp.float32)).astype(jnp.bfloat16)
        for a in range(per_group):
            cut = slice(a * c_blk, (a + 1) * c_blk)
            lane = slice(a * LANES, a * LANES + inner)
            rhs[:c_blk, lane] = w_high[cut]
            rhs[c_blk : 2 * c_blk, lane] = w_high[cut]
            rhs[2 * c_blk : 3 * c_blk, lane] = w_low[cut]
            rhs[3 * c_blk :, lane] = w_low[cut]
        fetch(i).wait()
        x = tbuf[lax.rem(i, DEPTH)].reshape(cols_j * cols_b, window)
        shift = lax.rem(off_ref[slot], window)
        lane = lax.broadcasted_iota(jnp.int32, x.shape, 1)
        if window == 2 * c_blk:
            twice = jnp.where((lane < c_blk) == (shift < c_blk), x, pltpu.roll(x, c_blk, 1))
        else:
            one = pltpu.roll(x, lax.rem(window - shift, window), 1)
            twice = jnp.where(lane < c_blk, one, pltpu.roll(one, c_blk, 1))
        high = twice.astype(jnp.bfloat16).astype(jnp.float32)
        both = jnp.where(lane < c_blk, high, twice - high).astype(jnp.bfloat16)
        both = both[:, : 2 * c_blk]
        lhs = jnp.concatenate([both, both], axis=1)
        prod = jnp.dot(lhs, rhs[...], preferred_element_type=jnp.float32)
        acc[...] += prod.reshape(acc.shape)

    if final:
        rows = out_ref.shape[1]
        for a in range(per_group):
            for b in range(cols_b):
                out_ref[a, :, b, :] = acc[:, b, a * LANES : (a + 1) * LANES].T[:rows]


def contract(sources, views, ent, off, amplitudes, c_blk, adds=(), final=None):
    _, cols_j, cols_b, _ = amplitudes.shape
    rows, lanes = sources[0].shape[-2:]
    per_group = lanes // c_blk
    slots = ent.shape[0]
    window = max(LANES, 2 * c_blk)
    held = jax.ShapeDtypeStruct((cols_j, cols_b, per_group * LANES), jnp.float32)
    smem = pl.BlockSpec(memory_space=pltpu.SMEM)
    hbm = pl.BlockSpec(memory_space=pl.ANY)
    vmem = pl.BlockSpec(memory_space=pltpu.VMEM)
    scratch = [
        pltpu.VMEM((slots, rows, lanes), jnp.float32),
        pltpu.VMEM((DEPTH, cols_j, cols_b, window), jnp.float32),
        pltpu.VMEM((4 * c_blk, per_group * LANES), jnp.bfloat16),
        pltpu.SMEM((slots,), jnp.int32),
        pltpu.SemaphoreType.DMA((len(sources),)),
        pltpu.SemaphoreType.DMA((DEPTH,)),
    ]
    if final is not None:
        scratch.append(pltpu.VMEM(held.shape, jnp.float32))
        held = jax.ShapeDtypeStruct((per_group, final, cols_b, cols_j), jnp.float32)
    return pl.pallas_call(
        functools.partial(contract_kernel, views, final is not None, c_blk, len(adds)),
        out_shape=held,
        in_specs=[smem, smem] + [hbm] * (len(sources) + 1) + [vmem] * len(adds),
        out_specs=vmem,
        scratch_shapes=scratch,
        compiler_params=pltpu.CompilerParams(vmem_limit_bytes=VMEM_LIMIT),
        cost_estimate=pl.CostEstimate(
            flops=slots * cols_j * cols_b * per_group * LANES * c_blk,
            bytes_accessed=slots * cols_j * cols_b * LANES * 2,
            transcendentals=0,
        ),
        name="contract_pairs",
    )(ent, off, *sources, amplitudes, *adds)


def body(integrals, amplitudes, occ_irreps, virt_irreps):
    k_local, c_local, rows_a, inner = integrals.shape
    groups = lax.axis_size("summa")
    parts = lax.axis_size("amp") * lax.axis_size("rep")
    me = lax.axis_index("summa")
    tile = parts * c_local // virt_irreps.shape[0]
    c_blk = min(tile, c_local)
    blocks = c_local // c_blk
    turned = jnp.transpose(amplitudes, (0, 3, 1, 2))

    occ = lax.dynamic_slice_in_dim(occ_irreps, me * k_local, k_local)
    block_labels = jnp.repeat(virt_irreps, tile // c_blk).reshape(parts, blocks)
    allowed = (occ[:, None, None] == block_labels.T[None]).reshape(k_local * blocks, parts)
    ranks = jnp.cumsum(allowed.astype(jnp.int32), axis=0)
    mine = lax.axis_index("amp") * lax.axis_size("rep") + lax.axis_index("rep")
    entry = jnp.arange(k_local * blocks, dtype=jnp.int32)

    def gather_round(start):
        wanted = start + 1 + jnp.arange(CAP, dtype=jnp.int32)
        hit = allowed[:, :, None] & (ranks[:, :, None] == wanted)
        ent = jnp.sum(jnp.where(hit, entry[:, None, None] + 1, 0), axis=0) - 1
        own = lax.dynamic_index_in_dim(ent, mine, keepdims=False)
        packed = pack(integrals, own, me[None], groups, c_blk)
        panel = lax.all_gather(packed, ("amp", "rep"))
        k_of = jnp.where(ent < 0, -1, ent // blocks).reshape(-1)
        off = jnp.arange(parts, dtype=jnp.int32)[:, None] * c_local + (ent % blocks) * c_blk
        off = jnp.where(ent < 0, 0, off).reshape(-1)
        received = []
        for phase in range(1, groups):
            views = [(d, phase) for d in range(parts)]
            value = contract([panel] * parts, views, k_of, off, turned, c_blk)
            received.append(lax.ppermute(value, "summa", [(i, (i + phase) % groups) for i in range(groups)]))
        views = [(d, 0) for d in range(parts)]
        return contract([panel] * parts, views, k_of, off, turned, c_blk, received, inner)

    everyone = (occ_irreps[:, None, None] == block_labels.T[None]).reshape(groups, -1, parts)
    most = lax.pmax(jnp.max(jnp.sum(everyone.astype(jnp.int32), axis=1)), "mol")
    first = gather_round(jnp.int32(0))

    def more(state):
        return state[0] < most

    def step(state):
        start, value = state
        return start + CAP, value + gather_round(start)

    return lax.while_loop(more, step, (jnp.int32(CAP), first))[1]


def solution(mesh):
    return jax.shard_map(
        body,
        mesh=mesh,
        in_specs=(
            P(("mol", "summa"), ("amp", "rep"), None, None),
            P(("mol", "summa"), ("amp", "rep"), None, None),
            P("mol"),
            P("mol"),
        ),
        out_specs=P(("mol", "summa"), None, ("amp", "rep"), None),
        check_vma=False,
    )
```

```python
import functools
import math

import jax
import jax.numpy as jnp
from jax import lax
from jax.experimental import pallas as pl
from jax.experimental.pallas import tpu as pltpu
from jax.sharding import PartitionSpec as P

CAP = 12
RING = 5
OWN = 16
DEPTH = 4
LANES = 128
VMEM_LIMIT = 60 * 1024 * 1024


def round_up(value, unit):
    return -(-value // unit) * unit


def pack_kernel(groups, tile, cuts, pos_ref, occ_ref, virt_ref, src_ref, *refs):
    outs, (buf, stage, sems, out_sems) = refs[:-4], refs[-4:]
    slots, c_blk, rows_a, inner = buf.shape
    k_local, c_local = src_ref.shape[:2]
    blocks = c_local // c_blk
    per_group = rows_a // groups
    me, mine, start = pos_ref[0], pos_ref[1], pos_ref[2]

    def look(ent, found):
        k, block = (ent, 0) if blocks == 1 else (ent // blocks, ent % blocks)
        same = occ_ref[me * k_local + k] == virt_ref[(mine * c_local + block * c_blk) // tile]
        slot = found - start

        @pl.when(same & (slot >= 0) & (slot < slots))
        def _():
            rows = pl.ds(pl.multiple_of(block * c_blk, c_blk), c_blk)
            pltpu.make_async_copy(src_ref.at[k, rows], buf.at[slot], sems.at[slot]).start()

        return found + same.astype(jnp.int32)

    found = lax.fori_loop(0, k_local * blocks, look, jnp.int32(0))

    @pl.loop(0, jnp.clip(found - start, 0, slots))
    def _(slot):
        pltpu.make_async_copy(src_ref.at[0, pl.ds(0, c_blk)], buf.at[slot], sems.at[slot]).wait()
        for a in range(rows_a):
            phase = lax.rem(a // per_group - me + groups, groups)
            lane = (a % per_group) * c_blk
            stage[phase, slot, :inner, lane : lane + c_blk] = buf[slot, :, a, :].T

    copies = []
    for i, (out, (first, last)) in enumerate(zip(outs, cuts)):
        view = stage.at[:, pl.ds(first, last - first)]
        copies.append(pltpu.make_async_copy(view, out, out_sems.at[i]))
        copies[-1].start()
    for one in copies:
        one.wait()


def pack(integrals, occ, virt, pos, groups, c_blk, tile, cuts):
    _, _, rows_a, inner = integrals.shape
    slots = cuts[-1][1]
    shape = (round_up(inner, 8), rows_a // groups * c_blk)
    smem = pl.BlockSpec(memory_space=pltpu.SMEM)
    hbm = pl.BlockSpec(memory_space=pltpu.HBM)
    return pl.pallas_call(
        functools.partial(pack_kernel, groups, tile, cuts),
        out_shape=[jax.ShapeDtypeStruct((groups, last - first) + shape, jnp.float32) for first, last in cuts],
        in_specs=[smem, smem, smem, hbm],
        out_specs=[hbm] * len(cuts),
        scratch_shapes=[
            pltpu.VMEM((slots, c_blk, rows_a, inner), jnp.float32),
            pltpu.VMEM((groups, slots) + shape, jnp.float32),
            pltpu.SemaphoreType.DMA((slots,)),
            pltpu.SemaphoreType.DMA((len(cuts),)),
        ],
        compiler_params=pltpu.CompilerParams(vmem_limit_bytes=VMEM_LIMIT),
        name="pack_pairs",
    )(pos, occ, virt, integrals)


def plan_kernel(chips, k_local, c_local, c_blk, tile, pos_ref, occ_ref, virt_ref, after_ref, out_ref, spares):
    del after_ref
    blocks = c_local // c_blk
    me, mine = pos_ref[0], pos_ref[1]
    z, core = mine // 2, lax.rem(mine, 2)

    @pl.loop(0, 2 * chips)
    def _(d):
        def look(ent, found):
            k, block = (ent, 0) if blocks == 1 else (ent // blocks, ent % blocks)
            same = occ_ref[me * k_local + k] == virt_ref[(d * c_local + block * c_blk) // tile]
            return found + same.astype(jnp.int32)

        spares[d] = jnp.maximum(lax.fori_loop(0, k_local * blocks, look, jnp.int32(0), unroll=5) - RING, 0)

    def share(chip):
        return (spares[2 * chip] + spares[2 * chip + 1] + 1 - core) // 2

    def add(chip, held):
        one = share(chip)
        return held[0] + jnp.where(chip >= z, one, 0), held[1] + jnp.where(chip <= z, one, 0)

    held = lax.fori_loop(0, chips, add, (jnp.int32(0), jnp.int32(0)))
    for h in range(1, chips):
        for way, sender in enumerate([chips - h, h - 1]):
            row = [core, spares[2 * z], share(z), jnp.where(z == sender, held[way], 0)]
            for i, value in enumerate(row):
                out_ref[((h - 1) * 2 + way) * 4 + i] = value


def plan(pos, occ, virt, after, chips, k_local, c_local, c_blk, tile):
    smem = pl.BlockSpec(memory_space=pltpu.SMEM)
    return pl.pallas_call(
        functools.partial(plan_kernel, chips, k_local, c_local, c_blk, tile),
        out_shape=jax.ShapeDtypeStruct(((chips - 1) * 8,), jnp.int32),
        in_specs=[smem, smem, smem, pl.BlockSpec(memory_space=pltpu.HBM)],
        out_specs=smem,
        scratch_shapes=[pltpu.SMEM((2 * chips,), jnp.int32)],
        name="plan_messages",
    )(pos, occ, virt, after)


def gate_kernel(n_got, n_held, n_out, split, hop, info_ref, own_ref, other_ref, *refs):
    got = refs[:n_got]
    outs = refs[n_got + n_held : n_got + n_held + n_out]
    stage, sems, out_sems = refs[-3:]
    cap = sems.shape[1]
    groups = own_ref.shape[0]
    if not n_out:
        return

    for step in range(2):
        for way in range(2):
            core, first_count, share, total = (info_ref[((hop - 1) * 2 + way) * 4 + i] for i in range(4))

            @pl.loop(0, jnp.minimum(total, cap))
            def _(slot):
                dst, sem = stage.at[way, :, slot], sems.at[way, slot]
                if step:
                    pltpu.make_async_copy(own_ref.at[:, 0], dst, sem).wait()
                    return
                place = 2 * slot + core
                second = (place >= first_count).astype(jnp.int32)
                rank = place - second * first_count

                @pl.when((slot < share) & (second == core))
                def _():
                    pltpu.make_async_copy(own_ref.at[:, rank], dst, sem).start()

                @pl.when((slot < share) & (second != core))
                def _():
                    pltpu.make_async_copy(other_ref.at[:, rank], dst, sem).start()

                if got:

                    @pl.when(slot >= share)
                    def _():
                        pltpu.make_async_copy(got[way].at[:, slot - share], dst, sem).start()

    def put(way, i):
        view = stage.at[way, i % groups] if split else stage.at[way]
        return pltpu.make_async_copy(view, outs[i], out_sems.at[i])

    for action in range(2):
        for i in range(n_out):
            way = i // groups if split else i

            @pl.when(info_ref[((hop - 1) * 2 + way) * 4 + 3] > 0)
            def _():
                put(way, i).wait() if action else put(way, i).start()


def gate(info, own, other, got, cap, split, held, hop=1):
    groups, _, *tile = own.shape
    hbm = pl.BlockSpec(memory_space=pltpu.HBM)
    out = [(cap, *tile)] * (2 * groups) if split else [(groups, cap, *tile)] * 2
    if not cap:
        out = []
    n_in = 3 + len(got)
    done = pl.pallas_call(
        functools.partial(gate_kernel, len(got), len(held), len(out), split, hop),
        out_shape=[jax.ShapeDtypeStruct(shape, jnp.float32) for shape in out]
        + [jax.ShapeDtypeStruct(one.shape, one.dtype) for one in held],
        in_specs=[pl.BlockSpec(memory_space=pltpu.SMEM)] + [hbm] * (n_in - 1 + len(held)),
        out_specs=[hbm] * (len(out) + len(held)),
        scratch_shapes=[
            pltpu.VMEM((2, groups, max(cap, 1), *tile), jnp.float32),
            pltpu.SemaphoreType.DMA((2, max(cap, 1))),
            pltpu.SemaphoreType.DMA((max(len(out), 1),)),
        ],
        input_output_aliases={n_in + i: len(out) + i for i in range(len(held))},
        compiler_params=pltpu.CompilerParams(vmem_limit_bytes=VMEM_LIMIT),
        name="next_step",
    )(info, own, other, *got, *held)
    return done[: len(out)], done[len(out) :]


def contract_kernel(views, final, c_blk, n_acc, width, ent_ref, off_ref, *refs):
    n_src = len(views)
    srcs, amp_ref, adds = refs[:n_src], refs[n_src], refs[n_src + 1 : n_src + 1 + n_acc]
    out_refs = refs[n_src + 1 + n_acc : n_src + 1 + n_acc + width]
    wall, tbuf, rhs, todo, held_at, found, wsem, tsem, *rest = refs[n_src + 1 + n_acc + width :]
    accs = rest if final else out_refs
    inner = wall.shape[2]
    _, shares, cols_j, cols_b, window = tbuf.shape
    per_group = accs[0].shape[2] // LANES

    for part in range(shares + 1):
        found[part] = 0
    for ref, (lead, start, count, base) in zip(srcs, views):

        @pl.loop(0, count)
        def _(slot, ref=ref, lead=lead, start=start, base=base):
            @pl.when(ent_ref[start + slot] >= 0)
            def _():
                part = lax.rem(off_ref[start + slot] // c_blk, shares)
                at, held = found[part], found[shares]
                todo[part, at] = start + slot
                held_at[part, at] = held
                found[part] = at + 1
                found[shares] = held + 1
                dst = wall.at[held] if width > 1 else wall.at[held, 0]
                pltpu.make_async_copy(ref.at[lead + (base + slot,)], dst, wsem.at[held]).start()

    counts = [found[part] for part in range(shares)]
    total = functools.reduce(jnp.maximum, counts)

    def fetch(i, part):
        slot = todo[part, i]
        place = lax.rem(i, DEPTH)
        first = pl.multiple_of((off_ref[slot] // window) * window, window)
        return pltpu.make_async_copy(
            amp_ref.at[ent_ref[slot], :, :, pl.ds(first, window)], tbuf.at[place, part], tsem.at[place, part]
        )

    def start(i):
        for part in range(shares):

            @pl.when(i < counts[part])
            def _():
                fetch(i, part).start()

    for i in range(DEPTH - 1):
        start(jnp.int32(i))
    rhs[...] = jnp.zeros_like(rhs)
    for n, acc in enumerate(accs):
        mine = adds[n::width]
        value = mine[0][...] if mine else jnp.zeros(acc.shape, jnp.float32)
        for one in mine[1:]:
            value += one[...]
        acc[...] = value

    @pl.loop(0, total)
    def _(i):
        start(i + DEPTH - 1)
        place = lax.rem(i, DEPTH)
        for part in range(shares):
            live = i < counts[part]
            held = jnp.where(live, held_at[part, i], 0)

            @pl.when(live)
            def _():
                dst = wall.at[held] if width > 1 else wall.at[held, 0]
                pltpu.make_async_copy(srcs[0].at[views[0][0] + (0,)], dst, wsem.at[held]).wait()

            for n in range(width):
                w = wall[held, n].T
                w = jnp.where(jnp.full(w.shape, i, jnp.int32) < counts[part], w, 0.0)
                for a in range(per_group):
                    one = w[a * c_blk : (a + 1) * c_blk]
                    high = one.astype(jnp.bfloat16)
                    low = (one - high.astype(jnp.float32)).astype(jnp.bfloat16)
                    lane = (n * per_group + a) * LANES
                    lane = slice(lane, lane + inner)
                    for copy, value in enumerate([high, high, low]):
                        row = copy * window + part * c_blk
                        rhs[row : row + c_blk, lane] = value
        x = jnp.zeros((cols_j * cols_b, window), jnp.float32)
        lane = lax.broadcasted_iota(jnp.int32, x.shape, 1)
        for part in range(shares):

            @pl.when(i < counts[part])
            def _():
                fetch(i, part).wait()

            limit = jnp.where(i < counts[part], (part + 1) * c_blk, 0)
            mask = (lane >= part * c_blk) & (lane < limit)
            x = jnp.where(mask, tbuf[place, part].reshape(x.shape), x)
        high = x.astype(jnp.bfloat16)
        low = (x - high.astype(jnp.float32)).astype(jnp.bfloat16)
        lhs = jnp.concatenate([high, low, high], axis=1)
        prod = jnp.dot(lhs, rhs[...], preferred_element_type=jnp.float32)
        for n, acc in enumerate(accs):
            lanes = per_group * LANES
            acc[...] += prod[:, n * lanes : (n + 1) * lanes].reshape(acc.shape)

    if final:
        (out_ref,), (acc,) = out_refs, accs
        rows = out_ref.shape[1]
        for a in range(per_group):
            for b in range(cols_b):
                out_ref[a, :, b, :] = acc[:, b, a * LANES : (a + 1) * LANES].T[:rows]


def contract(sources, views, ent, off, amplitudes, c_blk, adds=(), final=None, width=1):
    _, cols_j, cols_b, _ = amplitudes.shape
    rows, lanes = sources[0].shape[-2:]
    per_group = lanes // c_blk
    slots = sum(view[2] for view in views)
    window = max(LANES, c_blk)
    shares = window // c_blk
    held = [jax.ShapeDtypeStruct((cols_j, cols_b, per_group * LANES), jnp.float32)] * width
    smem = pl.BlockSpec(memory_space=pltpu.SMEM)
    hbm = pl.BlockSpec(memory_space=pltpu.HBM)
    vmem = pl.BlockSpec(memory_space=pltpu.VMEM)
    scratch = [
        pltpu.VMEM((slots, width, rows, lanes), jnp.float32),
        pltpu.VMEM((DEPTH, shares, cols_j, cols_b, window), jnp.float32),
        pltpu.VMEM((3 * window, width * per_group * LANES), jnp.bfloat16),
        pltpu.SMEM((shares, slots), jnp.int32),
        pltpu.SMEM((shares, slots), jnp.int32),
        pltpu.SMEM((shares + 1,), jnp.int32),
        pltpu.SemaphoreType.DMA((slots,)),
        pltpu.SemaphoreType.DMA((DEPTH, shares)),
    ]
    if final is not None:
        scratch.append(pltpu.VMEM(held[0].shape, jnp.float32))
        held = [jax.ShapeDtypeStruct((per_group, final, cols_b, cols_j), jnp.float32)]
    return pl.pallas_call(
        functools.partial(contract_kernel, views, final is not None, c_blk, len(adds), width),
        out_shape=held,
        in_specs=[smem, smem] + [hbm] * (len(sources) + 1) + [vmem] * len(adds),
        out_specs=[vmem] * width,
        scratch_shapes=scratch,
        compiler_params=pltpu.CompilerParams(vmem_limit_bytes=VMEM_LIMIT),
        cost_estimate=pl.CostEstimate(
            flops=width * slots * cols_j * cols_b * per_group * LANES * c_blk,
            bytes_accessed=slots * cols_j * cols_b * LANES * 2,
            transcendentals=0,
        ),
        name="contract_pairs",
    )(ent, off, *sources, amplitudes, *adds)


def spare_caps(hops, scale):
    return [math.ceil(scale * (2.0 * h + 4.3 * math.sqrt(h))) for h in range(1, hops + 1)]


def body(integrals, amplitudes, occ_irreps, virt_irreps):
    k_local, c_local, rows_a, inner = integrals.shape
    groups = lax.axis_size("summa")
    chips = lax.axis_size("amp")
    cores = lax.axis_size("rep")
    parts = chips * cores
    me = lax.axis_index("summa")
    z = lax.axis_index("amp")
    core = lax.axis_index("rep")
    mine = z * cores + core
    tile = parts * c_local // virt_irreps.shape[0]
    c_blk = min(tile, c_local)
    blocks = c_local // c_blk
    entries = k_local * blocks

    turned = jnp.transpose(amplitudes, (0, 3, 1, 2))
    entry = jnp.arange(entries, dtype=jnp.int32)
    device = jnp.arange(parts, dtype=jnp.int32)

    def swap(value):
        return lax.ppermute(value, "rep", [(0, 1), (1, 0)])

    ways = [-1, 1]

    def along(way, value, sources):
        return lax.ppermute(value, "amp", [(i, i + ways[way]) for i in sources])

    def packed(start, cuts):
        pos = jnp.stack([me, mine, jnp.asarray(start, jnp.int32)])
        return pos, pack(integrals, occ_irreps, virt_irreps, pos, groups, c_blk, tile, cuts)

    hops = chips - 1
    spare = OWN - RING
    caps = spare_caps(hops, entries / 50)
    pos, (ring, spares) = packed(0, [(0, RING), (RING, OWN)])
    info = plan(pos, occ_irreps, virt_irreps, ring, chips, k_local, c_local, c_blk, tile)
    sister_spares, sister_ring = swap(spares), swap(ring)
    last = [along(way, ring, [range(1, chips), range(chips - 1)][way]) for way in range(2)]
    held = [*last, ring, sister_ring]
    sent, held = gate(info, spares, sister_spares, [], caps[0], False, held)
    last, (ring, sister_ring) = held[:2], held[2:]

    occ = lax.dynamic_slice_in_dim(occ_irreps, me * k_local, k_local)
    block_labels = jnp.repeat(virt_irreps, tile // c_blk).reshape(parts, blocks)
    allowed = (occ[:, None, None] == block_labels.T[None]).reshape(entries, parts)
    ranks = jnp.cumsum(allowed.astype(jnp.int32), axis=0) - 1
    counts = ranks[-1] + 1

    def places(ident):
        ent, dev = ident // parts, ident % parts
        k_of = jnp.where(ident < 0, -1, ent // blocks)
        return k_of, jnp.where(ident < 0, 0, dev * c_local + (ent % blocks) * c_blk)

    def listed(where, count):
        hit = allowed[:, :, None] & (where[:, :, None] == jnp.arange(count, dtype=jnp.int32))
        ident = entry[:, None] * parts + device
        return jnp.sum(jnp.where(hit, ident[:, :, None] + 1, 0), axis=(0, 1)) - 1

    def across(value, shift):
        return lax.ppermute(value, "summa", [(i, (i + shift) % groups) for i in range(groups)])

    def gather_round(start):
        panel = lax.all_gather(packed(start, [(0, CAP)])[1][0], ("amp", "rep"))
        inside = (ranks >= start) & (ranks < start + CAP)
        k_of, off = places(listed(jnp.where(inside, ranks - start + device * CAP, -1), parts * CAP))
        received = []
        for phase in [*range(1, groups), 0]:
            views = [((d, phase), d * CAP, CAP, 0) for d in range(parts)]
            if phase:
                received.append(across(contract([panel] * parts, views, k_of, off, turned, c_blk)[0], phase))
        return contract([panel] * parts, views, k_of, off, turned, c_blk, received, inner)[0]

    every = (occ_irreps[:, None, None] == block_labels.T[None]).reshape(groups, entries, parts)
    every = jnp.sum(every.astype(jnp.int32), axis=1)
    spare_all = jnp.maximum(every - RING, 0).reshape(groups, chips, cores)
    share_all = (spare_all.sum(2)[:, :, None] + 1 - jnp.arange(2, dtype=jnp.int32)) // 2
    ahead_all = jnp.cumsum(share_all[:, ::-1], axis=1)[:, ::-1]
    behind_all = jnp.cumsum(share_all, axis=1)
    fits = jnp.max(every) <= OWN
    for h in range(1, hops + 1):
        fits &= (jnp.max(ahead_all[:, chips - h]) <= caps[h - 1]) & (jnp.max(behind_all[:, h - 1]) <= caps[h - 1])
    own_verdict = jnp.stack([1 - fits.astype(jnp.int32), jnp.max(every)])
    verdict = own_verdict
    mols = lax.axis_size("mol")
    for shift in range(1, mols):
        turn = [(i, (i + shift) % mols) for i in range(mols)]
        verdict = jnp.maximum(verdict, lax.ppermute(own_verdict, "mol", turn))
    over, share, ahead, behind = spare_all[me], share_all[me], ahead_all[me], behind_all[me]

    base_ring, base_own = 0, 2 * hops * cores * RING
    base_sister = base_own + OWN
    base_chain = [[0] * (hops + 1) for _ in range(2)]
    total = base_sister + OWN
    for h in range(1, hops + 1):
        for way in range(2):
            base_chain[way][h] = total
            total += 2 * caps[h - 1]
    cap_at = jnp.array([0] + caps, jnp.int32)
    base_at = jnp.array(base_chain, jnp.int32)
    chip_of, core_of = device // cores, device % cores
    dz = chip_of - z
    way = (dz < 0).astype(jnp.int32)
    sister = (core_of != core).astype(jnp.int32)
    at_ring = base_ring + ((way * hops + jnp.abs(dz) - 1) * 2 + sister) * RING + ranks
    combined = ranks - RING + jnp.where(core_of == 1, over[:, 0][chip_of], 0)
    lane = combined % 2
    between_l = jnp.where((jnp.arange(chips) > z)[:, None], share, 0)
    between_l = jnp.cumsum(between_l, axis=0) - between_l
    between_r = jnp.where((jnp.arange(chips) < z)[:, None], share, 0)
    between_r = jnp.cumsum(between_r[::-1], axis=0)[::-1] - between_r
    between = jnp.where(dz[:, None] > 0, between_l[chip_of], between_r[chip_of])
    hop_at = jnp.where(way == 1, z, chips - 1 - z)
    at_chain = (
        base_at[way, hop_at]
        + jnp.where(lane != core, cap_at[hop_at], 0)
        + combined // 2
        + jnp.where(lane == 1, between[:, 1], between[:, 0])
    )
    at_chip = jnp.where(sister == 1, base_sister, base_own) + ranks
    where = jnp.where(dz == 0, at_chip, jnp.where(ranks < RING, at_ring, at_chain))
    k_of, off = places(listed(where, total))

    def sums(sources, **more):
        return contract([one[0] for one in sources], [one[1:] for one in sources], k_of, off, turned, c_blk, **more)

    every_group = (slice(None),)

    def joined(h):
        slots = [((way * hops + h - 1) * 2 * RING, RING) for way in range(2)]
        values = list(rings[h - 1])
        if h > 1:
            slots += [(base_chain[way][h - 1], caps[h - 2]) for way in range(2)]
            values += chain[h - 2]
        out, base = [], 0
        for value, (start, count) in zip(values, slots):
            out.append((value, every_group, start, count, 0))
            if len(swapped[h - 1]) > 1:
                out.append((swapped[h - 1][len(out) // 2], every_group, start + count, count, 0))
            else:
                out.append((swapped[h - 1][0], every_group, start + count, count, base))
            base += count
        return out

    rings, chain, swapped = [last], [], []
    ready = [
        (ring, every_group, base_own, RING, 0),
        (spares, every_group, base_own + RING, spare, 0),
        (sister_ring, every_group, base_sister, RING, 0),
        (sister_spares, every_group, base_sister + RING, spare, 0),
    ]
    early = []
    for h in range(2, hops + 1):
        sources = [range(1, chips - h + 1), range(h - 1, chips - 1)]
        last = [along(way, last[way], sources[way]) for way in range(2)]
        new = [along(0, sent[0], [chips - h + 1]), along(1, sent[1], [h - 2])]
        if chain:
            other = [swap(jnp.concatenate([*rings[-1], *chain[-1]], axis=1))]
        else:
            other = [swap(one) for one in rings[-1]]
        early = sums(ready, adds=early, width=groups)
        sent, held = gate(info, spares, sister_spares, new, caps[h - 1], h == hops, [*last, *other, *early, verdict], h)
        last, early, verdict = held[:2], held[-1 - groups : -1], held[-1]
        swapped.append(held[2 : -1 - groups])
        ready = joined(h - 1)
        chain.append(new)
        rings.append(last)
    swapped.append([swap(jnp.concatenate([*rings[-1], *chain[-1]], axis=1))])
    early = sums(ready + joined(hops), adds=early, width=groups)
    order = [*range(1, groups), 0]
    received = []
    waiting = sent
    for n, phase in enumerate(order):
        final = [along(way, waiting[way * groups + phase], [[1], [hops - 1]][way]) for way in range(2)]
        if n + 1 < groups:
            held = [*final, *waiting, *early]
            _, held = gate(info, spares, sister_spares, [], 0, False, held)
            final, waiting, early = held[:2], held[2:-groups], held[-groups:]
        other = [swap(one) for one in final]
        sources = []
        for way in range(2):
            start, cap = base_chain[way][hops], caps[-1]
            sources += [(final[way], (), start, cap, 0), (other[way], (), start + cap, cap, 0)]
        if phase:
            received.append(across(sums(sources, adds=[early[phase]])[0], phase))
        else:
            (first,) = sums(sources, adds=[early[phase], *received], final=inner)

    failed, most = verdict[0], verdict[1]

    def more(state):
        return state[0] < most

    def step(state):
        start, value = state
        return start + CAP, jnp.where(start == 0, 0.0, value) + gather_round(start)

    return lax.while_loop(more, step, (jnp.where(failed > 0, 0, most), first))[1]


def solution(mesh):
    return jax.shard_map(
        body,
        mesh=mesh,
        in_specs=(
            P(("mol", "summa"), ("amp", "rep"), None, None),
            P(("mol", "summa"), ("amp", "rep"), None, None),
            P("mol"),
            P("mol"),
        ),
        out_specs=P(("mol", "summa"), None, ("amp", "rep"), None),
        check_vma=False,
    )
```

```python
import functools

import jax
import jax.numpy as jnp
from jax import lax
from jax.experimental import pallas as pl
from jax.experimental.pallas import tpu as pltpu
from jax.sharding import PartitionSpec as P

CAP = 12
SHARE = 11
OWN = 15
DEPTH = 4
LANES = 128
VMEM_LIMIT = 60 * 1024 * 1024


def round_up(value, unit):
    return -(-value // unit) * unit


def pack_kernel(groups, tile, cuts, pos_ref, occ_ref, virt_ref, src_ref, *refs):
    outs, (buf, stage, sems, out_sems) = refs[:-4], refs[-4:]
    slots, c_blk, rows_a, inner = buf.shape
    k_local, c_local = src_ref.shape[:2]
    blocks = c_local // c_blk
    per_group = rows_a // groups
    me, mine, start = pos_ref[0], pos_ref[1], pos_ref[2]

    def look(ent, found):
        k, block = (ent, 0) if blocks == 1 else (ent // blocks, ent % blocks)
        same = occ_ref[me * k_local + k] == virt_ref[(mine * c_local + block * c_blk) // tile]
        slot = found - start

        @pl.when(same & (slot >= 0) & (slot < slots))
        def _():
            rows = pl.ds(pl.multiple_of(block * c_blk, c_blk), c_blk)
            pltpu.make_async_copy(src_ref.at[k, rows], buf.at[slot], sems.at[slot]).start()

        return found + same.astype(jnp.int32)

    found = lax.fori_loop(0, k_local * blocks, look, jnp.int32(0))

    @pl.loop(0, jnp.clip(found - start, 0, slots))
    def _(slot):
        pltpu.make_async_copy(src_ref.at[0, pl.ds(0, c_blk)], buf.at[slot], sems.at[slot]).wait()
        for a in range(rows_a):
            phase = lax.rem(a // per_group - me + groups, groups)
            lane = (a % per_group) * c_blk
            stage[phase, slot, :inner, lane : lane + c_blk] = buf[slot, :, a, :].T

    copies = []
    for i, (out, (first, last)) in enumerate(zip(outs, cuts)):
        view = stage.at[:, pl.ds(first, last - first)]
        copies.append(pltpu.make_async_copy(view, out, out_sems.at[i]))
        copies[-1].start()
    for one in copies:
        one.wait()


def pack(integrals, occ, virt, pos, groups, c_blk, tile, cuts):
    _, _, rows_a, inner = integrals.shape
    slots = cuts[-1][1]
    shape = (round_up(inner, 8), rows_a // groups * c_blk)
    smem = pl.BlockSpec(memory_space=pltpu.SMEM)
    hbm = pl.BlockSpec(memory_space=pltpu.HBM)
    return pl.pallas_call(
        functools.partial(pack_kernel, groups, tile, cuts),
        out_shape=[jax.ShapeDtypeStruct((groups, last - first) + shape, jnp.float32) for first, last in cuts],
        in_specs=[smem, smem, smem, hbm],
        out_specs=[hbm] * len(cuts),
        scratch_shapes=[
            pltpu.VMEM((slots, c_blk, rows_a, inner), jnp.float32),
            pltpu.VMEM((groups, slots) + shape, jnp.float32),
            pltpu.SemaphoreType.DMA((slots,)),
            pltpu.SemaphoreType.DMA((len(cuts),)),
        ],
        compiler_params=pltpu.CompilerParams(vmem_limit_bytes=VMEM_LIMIT),
        name="pack_pairs",
    )(pos, occ, virt, integrals)


def split_kernel(k_local, c_local, c_blk, tile, pos_ref, occ_ref, virt_ref, own_ref, other_ref, *refs):
    outs, (stage, sems, out_sems) = refs[:-3], refs[-3:]
    blocks = c_local // c_blk
    me, mine = pos_ref[0], pos_ref[1]
    core = lax.rem(mine, 2)

    def count(d):
        def look(ent, found):
            k, block = (ent, 0) if blocks == 1 else (ent // blocks, ent % blocks)
            same = occ_ref[me * k_local + k] == virt_ref[(d * c_local + block * c_blk) // tile]
            return found + same.astype(jnp.int32)

        return lax.fori_loop(0, k_local * blocks, look, jnp.int32(0), unroll=5)

    slots, most = stage.shape[1], own_ref.shape[1]
    first_count = count(mine - core)
    both = first_count + count(mine - core + 1)
    share = jnp.minimum((both + 1 - core) // 2, slots)
    for step in range(2):

        @pl.loop(0, share)
        def _(slot):
            dst, sem = stage.at[:, slot], sems.at[slot]
            if step:
                pltpu.make_async_copy(own_ref.at[:, 0], dst, sem).wait()
                return
            place = 2 * slot + core
            second = (place >= first_count).astype(jnp.int32)
            rank = jnp.minimum(place - second * first_count, most - 1)

            @pl.when(second == core)
            def _():
                pltpu.make_async_copy(own_ref.at[:, rank], dst, sem).start()

            @pl.when(second != core)
            def _():
                pltpu.make_async_copy(other_ref.at[:, rank], dst, sem).start()

    copies = [pltpu.make_async_copy(stage.at[n], out, out_sems.at[n]) for n, out in enumerate(outs)]
    for one in copies:
        one.start()
    for one in copies:
        one.wait()


def split(pos, occ, virt, own, other, k_local, c_local, c_blk, tile):
    groups, _, *shape = own.shape
    smem = pl.BlockSpec(memory_space=pltpu.SMEM)
    hbm = pl.BlockSpec(memory_space=pltpu.HBM)
    return pl.pallas_call(
        functools.partial(split_kernel, k_local, c_local, c_blk, tile),
        out_shape=[jax.ShapeDtypeStruct((SHARE, *shape), jnp.float32)] * groups,
        in_specs=[smem] * 3 + [hbm] * 2,
        out_specs=[hbm] * groups,
        scratch_shapes=[
            pltpu.VMEM((groups, SHARE, *shape), jnp.float32),
            pltpu.SemaphoreType.DMA((SHARE,)),
            pltpu.SemaphoreType.DMA((groups,)),
        ],
        compiler_params=pltpu.CompilerParams(vmem_limit_bytes=VMEM_LIMIT),
        name="split_pairs",
    )(pos, occ, virt, own, other)


def contract_kernel(views, final, c_blk, n_acc, width, ent_ref, off_ref, *refs):
    n_src = len(views)
    srcs, amp_ref, adds = refs[:n_src], refs[n_src], refs[n_src + 1 : n_src + 1 + n_acc]
    out_refs = refs[n_src + 1 + n_acc : n_src + 1 + n_acc + width]
    wall, tbuf, rhs, todo, held_at, found, wsem, tsem, *rest = refs[n_src + 1 + n_acc + width :]
    accs = rest if final else out_refs
    inner = wall.shape[2]
    _, shares, cols_j, cols_b, window = tbuf.shape
    per_group = accs[0].shape[2] // LANES

    for part in range(shares + 1):
        found[part] = 0
    for ref, (lead, start, count, base) in zip(srcs, views):

        @pl.loop(0, count)
        def _(slot, ref=ref, lead=lead, start=start, base=base):
            @pl.when(ent_ref[start + slot] >= 0)
            def _():
                part = lax.rem(off_ref[start + slot] // c_blk, shares)
                at, held = found[part], found[shares]
                todo[part, at] = start + slot
                held_at[part, at] = held
                found[part] = at + 1
                found[shares] = held + 1
                dst = wall.at[held] if width > 1 else wall.at[held, 0]
                pltpu.make_async_copy(ref.at[lead + (base + slot,)], dst, wsem.at[held]).start()

    counts = [found[part] for part in range(shares)]
    total = functools.reduce(jnp.maximum, counts)

    def fetch(i, part):
        slot = todo[part, i]
        place = lax.rem(i, DEPTH)
        first = pl.multiple_of((off_ref[slot] // window) * window, window)
        return pltpu.make_async_copy(
            amp_ref.at[ent_ref[slot], :, :, pl.ds(first, window)], tbuf.at[place, part], tsem.at[place, part]
        )

    def start(i):
        for part in range(shares):

            @pl.when(i < counts[part])
            def _():
                fetch(i, part).start()

    for i in range(DEPTH - 1):
        start(jnp.int32(i))
    rhs[...] = jnp.zeros_like(rhs)
    for n, acc in enumerate(accs):
        mine = adds[n::width]
        value = mine[0][...] if mine else jnp.zeros(acc.shape, jnp.float32)
        for one in mine[1:]:
            value += one[...]
        acc[...] = value

    @pl.loop(0, total)
    def _(i):
        start(i + DEPTH - 1)
        place = lax.rem(i, DEPTH)
        for part in range(shares):
            live = i < counts[part]
            held = jnp.where(live, held_at[part, i], 0)

            @pl.when(live)
            def _():
                dst = wall.at[held] if width > 1 else wall.at[held, 0]
                pltpu.make_async_copy(srcs[0].at[views[0][0] + (0,)], dst, wsem.at[held]).wait()

            for n in range(width):
                w = wall[held, n].T
                w = jnp.where(jnp.full(w.shape, i, jnp.int32) < counts[part], w, 0.0)
                for a in range(per_group):
                    one = w[a * c_blk : (a + 1) * c_blk]
                    high = one.astype(jnp.bfloat16)
                    low = (one - high.astype(jnp.float32)).astype(jnp.bfloat16)
                    lane = (n * per_group + a) * LANES
                    lane = slice(lane, lane + inner)
                    for copy, value in enumerate([high, high, low]):
                        row = copy * window + part * c_blk
                        rhs[row : row + c_blk, lane] = value
        x = jnp.zeros((cols_j * cols_b, window), jnp.float32)
        lane = lax.broadcasted_iota(jnp.int32, x.shape, 1)
        for part in range(shares):

            @pl.when(i < counts[part])
            def _():
                fetch(i, part).wait()

            limit = jnp.where(i < counts[part], (part + 1) * c_blk, 0)
            mask = (lane >= part * c_blk) & (lane < limit)
            x = jnp.where(mask, tbuf[place, part].reshape(x.shape), x)
        high = x.astype(jnp.bfloat16)
        low = (x - high.astype(jnp.float32)).astype(jnp.bfloat16)
        lhs = jnp.concatenate([high, low, high], axis=1)
        prod = jnp.dot(lhs, rhs[...], preferred_element_type=jnp.float32)
        for n, acc in enumerate(accs):
            lanes = per_group * LANES
            acc[...] += prod[:, n * lanes : (n + 1) * lanes].reshape(acc.shape)

    if final:
        (out_ref,), (acc,) = out_refs, accs
        rows = out_ref.shape[1]
        for a in range(per_group):
            for b in range(cols_b):
                out_ref[a, :, b, :] = acc[:, b, a * LANES : (a + 1) * LANES].T[:rows]


def contract(sources, views, ent, off, amplitudes, c_blk, adds=(), final=None, width=1):
    _, cols_j, cols_b, _ = amplitudes.shape
    rows, lanes = sources[0].shape[-2:]
    per_group = lanes // c_blk
    slots = max(1, sum(view[2] for view in views))
    window = max(LANES, c_blk)
    shares = window // c_blk
    held = [jax.ShapeDtypeStruct((cols_j, cols_b, per_group * LANES), jnp.float32)] * width
    smem = pl.BlockSpec(memory_space=pltpu.SMEM)
    hbm = pl.BlockSpec(memory_space=pltpu.HBM)
    vmem = pl.BlockSpec(memory_space=pltpu.VMEM)
    scratch = [
        pltpu.VMEM((slots, width, rows, lanes), jnp.float32),
        pltpu.VMEM((DEPTH, shares, cols_j, cols_b, window), jnp.float32),
        pltpu.VMEM((3 * window, width * per_group * LANES), jnp.bfloat16),
        pltpu.SMEM((shares, slots), jnp.int32),
        pltpu.SMEM((shares, slots), jnp.int32),
        pltpu.SMEM((shares + 1,), jnp.int32),
        pltpu.SemaphoreType.DMA((slots,)),
        pltpu.SemaphoreType.DMA((DEPTH, shares)),
    ]
    if final is not None:
        scratch.append(pltpu.VMEM(held[0].shape, jnp.float32))
        held = [jax.ShapeDtypeStruct((per_group, final, cols_b, cols_j), jnp.float32)]
    return pl.pallas_call(
        functools.partial(contract_kernel, views, final is not None, c_blk, len(adds), width),
        out_shape=held,
        in_specs=[smem, smem] + [hbm] * (len(sources) + 1) + [vmem] * len(adds),
        out_specs=[vmem] * width,
        scratch_shapes=scratch,
        compiler_params=pltpu.CompilerParams(vmem_limit_bytes=VMEM_LIMIT),
        cost_estimate=pl.CostEstimate(
            flops=width * slots * cols_j * cols_b * per_group * LANES * c_blk,
            bytes_accessed=slots * cols_j * cols_b * LANES * 2,
            transcendentals=0,
        ),
        name="contract_pairs",
    )(ent, off, *sources, amplitudes, *adds)


def together(held, after):
    hbm = pl.BlockSpec(memory_space=pltpu.HBM)
    return pl.pallas_call(
        lambda *refs: None,
        out_shape=[jax.ShapeDtypeStruct(one.shape, one.dtype) for one in held],
        in_specs=[hbm] * (len(held) + len(after)),
        out_specs=[hbm] * len(held),
        input_output_aliases={i: i for i in range(len(held))},
        name="together",
    )(*held, *after)


def body(integrals, amplitudes, occ_irreps, virt_irreps):
    k_local, c_local, rows_a, inner = integrals.shape
    groups = lax.axis_size("summa")
    chips = lax.axis_size("amp")
    cores = lax.axis_size("rep")
    parts = chips * cores
    me = lax.axis_index("summa")
    z = lax.axis_index("amp")
    core = lax.axis_index("rep")
    mine = z * cores + core
    tile = parts * c_local // virt_irreps.shape[0]
    c_blk = min(tile, c_local)
    blocks = c_local // c_blk
    entries = k_local * blocks

    turned = jnp.transpose(amplitudes, (0, 3, 1, 2))
    entry = jnp.arange(entries, dtype=jnp.int32)
    device = jnp.arange(parts, dtype=jnp.int32)

    def swap(value):
        return lax.ppermute(value, "rep", [(0, 1), (1, 0)])

    ways = [-1, 1]

    def along(way, value, sources):
        return lax.ppermute(value, "amp", [(i, i + ways[way]) for i in sources])

    def packed(start, cuts):
        pos = jnp.stack([me, mine, jnp.asarray(start, jnp.int32)])
        return pos, pack(integrals, occ_irreps, virt_irreps, pos, groups, c_blk, tile, cuts)

    hops = chips - 1
    pos, (own,) = packed(0, [(0, OWN)])
    sister_own = swap(own)
    halves = split(pos, occ_irreps, virt_irreps, own, sister_own, k_local, c_local, c_blk, tile)

    occ = lax.dynamic_slice_in_dim(occ_irreps, me * k_local, k_local)
    block_labels = jnp.repeat(virt_irreps, tile // c_blk).reshape(parts, blocks)
    allowed = (occ[:, None, None] == block_labels.T[None]).reshape(entries, parts)
    ranks = jnp.cumsum(allowed.astype(jnp.int32), axis=0) - 1
    counts = ranks[-1] + 1

    def places(ident):
        ent, dev = ident // parts, ident % parts
        k_of = jnp.where(ident < 0, -1, ent // blocks)
        return k_of, jnp.where(ident < 0, 0, dev * c_local + (ent % blocks) * c_blk)

    def listed(where, count):
        hit = allowed[:, :, None] & (where[:, :, None] == jnp.arange(count, dtype=jnp.int32))
        ident = entry[:, None] * parts + device
        return jnp.sum(jnp.where(hit, ident[:, :, None] + 1, 0), axis=(0, 1)) - 1

    def across(value, shift):
        return lax.ppermute(value, "summa", [(i, (i + shift) % groups) for i in range(groups)])

    def gather_round(start):
        panel = lax.all_gather(packed(start, [(0, CAP)])[1][0], ("amp", "rep"))
        inside = (ranks >= start) & (ranks < start + CAP)
        k_of, off = places(listed(jnp.where(inside, ranks - start + device * CAP, -1), parts * CAP))
        received = []
        for phase in [*range(1, groups), 0]:
            views = [((d, phase), d * CAP, CAP, 0) for d in range(parts)]
            if phase:
                received.append(across(contract([panel] * parts, views, k_of, off, turned, c_blk)[0], phase))
        return contract([panel] * parts, views, k_of, off, turned, c_blk, received, inner)[0]

    every = (occ_irreps[:, None, None] == block_labels.T[None]).reshape(groups, entries, parts)
    every = jnp.sum(every.astype(jnp.int32), axis=1)
    in_chip = jnp.max(every.reshape(groups, chips, cores).sum(2))
    fits = (jnp.max(every) <= OWN) & (in_chip <= 2 * SHARE)
    own_verdict = jnp.stack([1 - fits.astype(jnp.int32), jnp.max(every)])
    verdict = own_verdict
    mols = lax.axis_size("mol")
    for shift in range(1, mols):
        turn = [(i, (i + shift) % mols) for i in range(mols)]
        verdict = jnp.maximum(verdict, lax.ppermute(own_verdict, "mol", turn))

    base_hops = 2 * OWN
    total = base_hops + 2 * hops * 2 * SHARE
    dz = device // cores - z
    way = (dz < 0).astype(jnp.int32)
    first_count = jnp.repeat(counts.reshape(chips, cores)[:, 0], cores)
    combined = ranks + jnp.where(device % cores == 1, first_count, 0)
    sister = (combined % 2 != core).astype(jnp.int32)
    at_hop = base_hops + ((way * hops + jnp.abs(dz) - 1) * 2 + sister) * SHARE + combined // 2
    where = jnp.where(dz == 0, jnp.where(device % cores == core, 0, OWN) + ranks, at_hop)
    k_of, off = places(listed(where, total))

    def sums(sources, **more):
        return contract([one[0] for one in sources], [one[1:] for one in sources], k_of, off, turned, c_blk, **more)

    order = [*range(1, groups), 0]
    moved = {phase: [None] for phase in order}
    swapped = {phase: [None] for phase in order}

    def send(phase, values):
        h = len(moved[phase])
        sources = [range(1, chips - h + 1), range(h - 1, chips - 1)]
        moved[phase].append([along(way, values[way], sources[way]) for way in range(2)])

    def from_hop(h, phase):
        out = []
        for way in range(2):
            start = base_hops + (way * hops + h - 1) * 2 * SHARE
            out.append((moved[phase][h][way], (), start, SHARE, 0))
            out.append((swapped[phase][h][way], (), start + SHARE, SHARE, 0))
        return out

    for phase in order:
        send(phase, [halves[phase]] * 2)
    near = [(own, (slice(None),), 0, OWN, 0), (sister_own, (slice(None),), OWN, OWN, 0)]
    near = sums(near, width=groups)
    part = {phase: [near[phase]] for phase in order}
    for h in range(1, hops):
        for phase in order:
            if h > 1:
                part[phase] = sums(from_hop(h - 1, phase), adds=part[phase])
            here = together(moved[phase][h], part[phase])
            moved[phase][h] = here
            swapped[phase].append([swap(one) for one in here])
            send(phase, here)
    received = []
    for phase in order:
        swapped[phase].append([swap(one) for one in moved[phase][hops]])
        if hops > 1:
            part[phase] = sums(from_hop(hops - 1, phase), adds=part[phase])
        last = sums(from_hop(hops, phase), adds=part[phase])
        if phase:
            received.append(across(last[0], phase))
    (first,) = sums([(own, (0,), 0, 0, 0)], adds=[*last, *received], final=inner)

    failed, most = verdict[0], verdict[1]

    def more(state):
        return state[0] < most

    def step(state):
        start, value = state
        return start + CAP, jnp.where(start == 0, 0.0, value) + gather_round(start)

    return lax.while_loop(more, step, (jnp.where(failed > 0, 0, most), first))[1]


def solution(mesh):
    return jax.shard_map(
        body,
        mesh=mesh,
        in_specs=(
            P(("mol", "summa"), ("amp", "rep"), None, None),
            P(("mol", "summa"), ("amp", "rep"), None, None),
            P("mol"),
            P("mol"),
        ),
        out_specs=P(("mol", "summa"), None, ("amp", "rep"), None),
        check_vma=False,
    )
```

```python
import functools

import jax
import jax.numpy as jnp
from jax import lax
from jax.experimental import pallas as pl
from jax.experimental.pallas import tpu as pltpu
from jax.sharding import PartitionSpec as P

CAP = 12
SHARE = 11
OWN = 15
DEPTH = 4
LANES = 128
VMEM_LIMIT = 60 * 1024 * 1024


def round_up(value, unit):
    return -(-value // unit) * unit


def pack_kernel(groups, tile, cuts, pos_ref, occ_ref, virt_ref, src_ref, *refs):
    outs, (buf, stage, sems, out_sems) = refs[:-4], refs[-4:]
    slots, c_blk, rows_a, inner = buf.shape
    k_local, c_local = src_ref.shape[:2]
    blocks = c_local // c_blk
    per_group = rows_a // groups
    me, mine, start = pos_ref[0], pos_ref[1], pos_ref[2]

    def look(ent, found):
        k, block = (ent, 0) if blocks == 1 else (ent // blocks, ent % blocks)
        same = occ_ref[me * k_local + k] == virt_ref[(mine * c_local + block * c_blk) // tile]
        slot = found - start

        @pl.when(same & (slot >= 0) & (slot < slots))
        def _():
            rows = pl.ds(pl.multiple_of(block * c_blk, c_blk), c_blk)
            pltpu.make_async_copy(src_ref.at[k, rows], buf.at[slot], sems.at[slot]).start()

        return found + same.astype(jnp.int32)

    found = lax.fori_loop(0, k_local * blocks, look, jnp.int32(0))

    @pl.loop(0, jnp.clip(found - start, 0, slots))
    def _(slot):
        pltpu.make_async_copy(src_ref.at[0, pl.ds(0, c_blk)], buf.at[slot], sems.at[slot]).wait()
        for a in range(rows_a):
            phase = lax.rem(a // per_group - me + groups, groups)
            lane = (a % per_group) * c_blk
            stage[phase, slot, :inner, lane : lane + c_blk] = buf[slot, :, a, :].T

    copies = []
    for i, (out, (first, last)) in enumerate(zip(outs, cuts)):
        view = stage.at[:, pl.ds(first, last - first)]
        copies.append(pltpu.make_async_copy(view, out, out_sems.at[i]))
        copies[-1].start()
    for one in copies:
        one.wait()


def pack(integrals, occ, virt, pos, groups, c_blk, tile, cuts):
    _, _, rows_a, inner = integrals.shape
    slots = cuts[-1][1]
    shape = (round_up(inner, 8), rows_a // groups * c_blk)
    smem = pl.BlockSpec(memory_space=pltpu.SMEM)
    hbm = pl.BlockSpec(memory_space=pltpu.HBM)
    return pl.pallas_call(
        functools.partial(pack_kernel, groups, tile, cuts),
        out_shape=[jax.ShapeDtypeStruct((groups, last - first) + shape, jnp.float32) for first, last in cuts],
        in_specs=[smem, smem, smem, hbm],
        out_specs=[hbm] * len(cuts),
        scratch_shapes=[
            pltpu.VMEM((slots, c_blk, rows_a, inner), jnp.float32),
            pltpu.VMEM((groups, slots) + shape, jnp.float32),
            pltpu.SemaphoreType.DMA((slots,)),
            pltpu.SemaphoreType.DMA((len(cuts),)),
        ],
        compiler_params=pltpu.CompilerParams(vmem_limit_bytes=VMEM_LIMIT),
        name="pack_pairs",
    )(pos, occ, virt, integrals)


def split_kernel(k_local, c_local, c_blk, tile, pos_ref, occ_ref, virt_ref, own_ref, other_ref, *refs):
    outs, (stage, sems, out_sems) = refs[:-3], refs[-3:]
    blocks = c_local // c_blk
    me, mine = pos_ref[0], pos_ref[1]
    core = lax.rem(mine, 2)

    def count(d):
        def look(ent, found):
            k, block = (ent, 0) if blocks == 1 else (ent // blocks, ent % blocks)
            same = occ_ref[me * k_local + k] == virt_ref[(d * c_local + block * c_blk) // tile]
            return found + same.astype(jnp.int32)

        return lax.fori_loop(0, k_local * blocks, look, jnp.int32(0), unroll=5)

    slots, most = stage.shape[1], own_ref.shape[1]
    first_count = count(mine - core)
    both = first_count + count(mine - core + 1)
    share = jnp.minimum((both + 1 - core) // 2, slots)
    for step in range(2):

        @pl.loop(0, share)
        def _(slot):
            dst, sem = stage.at[:, slot], sems.at[slot]
            if step:
                pltpu.make_async_copy(own_ref.at[:, 0], dst, sem).wait()
                return
            place = 2 * slot + core
            second = (place >= first_count).astype(jnp.int32)
            rank = jnp.minimum(place - second * first_count, most - 1)

            @pl.when(second == core)
            def _():
                pltpu.make_async_copy(own_ref.at[:, rank], dst, sem).start()

            @pl.when(second != core)
            def _():
                pltpu.make_async_copy(other_ref.at[:, rank], dst, sem).start()

    copies = [pltpu.make_async_copy(stage.at[n], out, out_sems.at[n]) for n, out in enumerate(outs)]
    for one in copies:
        one.start()
    for one in copies:
        one.wait()


def split(pos, occ, virt, own, other, k_local, c_local, c_blk, tile):
    groups, _, *shape = own.shape
    smem = pl.BlockSpec(memory_space=pltpu.SMEM)
    hbm = pl.BlockSpec(memory_space=pltpu.HBM)
    return pl.pallas_call(
        functools.partial(split_kernel, k_local, c_local, c_blk, tile),
        out_shape=[jax.ShapeDtypeStruct((SHARE, *shape), jnp.float32)] * groups,
        in_specs=[smem] * 3 + [hbm] * 2,
        out_specs=[hbm] * groups,
        scratch_shapes=[
            pltpu.VMEM((groups, SHARE, *shape), jnp.float32),
            pltpu.SemaphoreType.DMA((SHARE,)),
            pltpu.SemaphoreType.DMA((groups,)),
        ],
        compiler_params=pltpu.CompilerParams(vmem_limit_bytes=VMEM_LIMIT),
        name="split_pairs",
    )(pos, occ, virt, own, other)


def contract_kernel(views, final, c_blk, n_acc, width, ent_ref, off_ref, *refs):
    n_src = len(views)
    srcs, amp_ref, adds = refs[:n_src], refs[n_src], refs[n_src + 1 : n_src + 1 + n_acc]
    out_refs = refs[n_src + 1 + n_acc : n_src + 1 + n_acc + width]
    wall, tbuf, rhs, todo, held_at, found, wsem, tsem, *rest = refs[n_src + 1 + n_acc + width :]
    accs = rest if final else out_refs
    inner = wall.shape[2]
    _, shares, cols_j, cols_b, window = tbuf.shape
    per_group = accs[0].shape[2] // LANES

    for part in range(shares + 1):
        found[part] = 0
    for ref, (lead, start, count, base) in zip(srcs, views):

        @pl.loop(0, count)
        def _(slot, ref=ref, lead=lead, start=start, base=base):
            @pl.when(ent_ref[start + slot] >= 0)
            def _():
                part = lax.rem(off_ref[start + slot] // c_blk, shares)
                at, held = found[part], found[shares]
                todo[part, at] = start + slot
                held_at[part, at] = held
                found[part] = at + 1
                found[shares] = held + 1
                dst = wall.at[held] if width > 1 else wall.at[held, 0]
                pltpu.make_async_copy(ref.at[lead + (base + slot,)], dst, wsem.at[held]).start()

    counts = [found[part] for part in range(shares)]
    total = functools.reduce(jnp.maximum, counts)

    def fetch(i, part):
        slot = todo[part, i]
        place = lax.rem(i, DEPTH)
        first = pl.multiple_of((off_ref[slot] // window) * window, window)
        return pltpu.make_async_copy(
            amp_ref.at[ent_ref[slot], :, :, pl.ds(first, window)], tbuf.at[place, part], tsem.at[place, part]
        )

    def start(i):
        for part in range(shares):

            @pl.when(i < counts[part])
            def _():
                fetch(i, part).start()

    for i in range(DEPTH - 1):
        start(jnp.int32(i))
    rhs[...] = jnp.zeros_like(rhs)
    for n, acc in enumerate(accs):
        mine = adds[n::width]
        value = mine[0][...] if mine else jnp.zeros(acc.shape, jnp.float32)
        for one in mine[1:]:
            value += one[...]
        acc[...] = value

    @pl.loop(0, total)
    def _(i):
        start(i + DEPTH - 1)
        place = lax.rem(i, DEPTH)
        for part in range(shares):
            live = i < counts[part]
            held = jnp.where(live, held_at[part, i], 0)

            @pl.when(live)
            def _():
                dst = wall.at[held] if width > 1 else wall.at[held, 0]
                pltpu.make_async_copy(srcs[0].at[views[0][0] + (0,)], dst, wsem.at[held]).wait()

            for n in range(width):
                w = wall[held, n].T
                w = jnp.where(jnp.full(w.shape, i, jnp.int32) < counts[part], w, 0.0)
                for a in range(per_group):
                    one = w[a * c_blk : (a + 1) * c_blk]
                    high = one.astype(jnp.bfloat16)
                    low = (one - high.astype(jnp.float32)).astype(jnp.bfloat16)
                    lane = (n * per_group + a) * LANES
                    lane = slice(lane, lane + inner)
                    for copy, value in enumerate([high, high, low]):
                        row = copy * window + part * c_blk
                        rhs[row : row + c_blk, lane] = value
        x = jnp.zeros((cols_j * cols_b, window), jnp.float32)
        lane = lax.broadcasted_iota(jnp.int32, x.shape, 1)
        for part in range(shares):

            @pl.when(i < counts[part])
            def _():
                fetch(i, part).wait()

            limit = jnp.where(i < counts[part], (part + 1) * c_blk, 0)
            mask = (lane >= part * c_blk) & (lane < limit)
            x = jnp.where(mask, tbuf[place, part].reshape(x.shape), x)
        high = x.astype(jnp.bfloat16)
        low = (x - high.astype(jnp.float32)).astype(jnp.bfloat16)
        lhs = jnp.concatenate([high, low, high], axis=1)
        prod = jnp.dot(lhs, rhs[...], preferred_element_type=jnp.float32)
        for n, acc in enumerate(accs):
            lanes = per_group * LANES
            acc[...] += prod[:, n * lanes : (n + 1) * lanes].reshape(acc.shape)

    if final:
        (out_ref,), (acc,) = out_refs, accs
        rows = out_ref.shape[1]
        for a in range(per_group):
            for b in range(cols_b):
                out_ref[a, :, b, :] = acc[:, b, a * LANES : (a + 1) * LANES].T[:rows]


def contract(sources, views, ent, off, amplitudes, c_blk, adds=(), final=None, width=1):
    _, cols_j, cols_b, _ = amplitudes.shape
    rows, lanes = sources[0].shape[-2:]
    per_group = lanes // c_blk
    slots = max(1, sum(view[2] for view in views))
    window = max(LANES, c_blk)
    shares = window // c_blk
    held = [jax.ShapeDtypeStruct((cols_j, cols_b, per_group * LANES), jnp.float32)] * width
    smem = pl.BlockSpec(memory_space=pltpu.SMEM)
    hbm = pl.BlockSpec(memory_space=pltpu.HBM)
    vmem = pl.BlockSpec(memory_space=pltpu.VMEM)
    scratch = [
        pltpu.VMEM((slots, width, rows, lanes), jnp.float32),
        pltpu.VMEM((DEPTH, shares, cols_j, cols_b, window), jnp.float32),
        pltpu.VMEM((3 * window, width * per_group * LANES), jnp.bfloat16),
        pltpu.SMEM((shares, slots), jnp.int32),
        pltpu.SMEM((shares, slots), jnp.int32),
        pltpu.SMEM((shares + 1,), jnp.int32),
        pltpu.SemaphoreType.DMA((slots,)),
        pltpu.SemaphoreType.DMA((DEPTH, shares)),
    ]
    if final is not None:
        scratch.append(pltpu.VMEM(held[0].shape, jnp.float32))
        held = [jax.ShapeDtypeStruct((per_group, final, cols_b, cols_j), jnp.float32)]
    return pl.pallas_call(
        functools.partial(contract_kernel, views, final is not None, c_blk, len(adds), width),
        out_shape=held,
        in_specs=[smem, smem] + [hbm] * (len(sources) + 1) + [vmem] * len(adds),
        out_specs=[vmem] * width,
        scratch_shapes=scratch,
        compiler_params=pltpu.CompilerParams(vmem_limit_bytes=VMEM_LIMIT),
        cost_estimate=pl.CostEstimate(
            flops=width * slots * cols_j * cols_b * per_group * LANES * c_blk,
            bytes_accessed=slots * cols_j * cols_b * LANES * 2,
            transcendentals=0,
        ),
        name="contract_pairs",
    )(ent, off, *sources, amplitudes, *adds)


def together(held, after):
    hbm = pl.BlockSpec(memory_space=pltpu.HBM)
    return pl.pallas_call(
        lambda *refs: None,
        out_shape=[jax.ShapeDtypeStruct(one.shape, one.dtype) for one in held],
        in_specs=[hbm] * (len(held) + len(after)),
        out_specs=[hbm] * len(held),
        input_output_aliases={i: i for i in range(len(held))},
        name="together",
    )(*held, *after)


def body(integrals, amplitudes, occ_irreps, virt_irreps):
    k_local, c_local, rows_a, inner = integrals.shape
    groups = lax.axis_size("summa")
    chips = lax.axis_size("amp")
    cores = lax.axis_size("rep")
    parts = chips * cores
    me = lax.axis_index("summa")
    z = lax.axis_index("amp")
    core = lax.axis_index("rep")
    mine = z * cores + core
    tile = parts * c_local // virt_irreps.shape[0]
    c_blk = min(tile, c_local)
    blocks = c_local // c_blk
    entries = k_local * blocks

    turned = jnp.transpose(amplitudes, (0, 3, 1, 2))
    entry = jnp.arange(entries, dtype=jnp.int32)
    device = jnp.arange(parts, dtype=jnp.int32)

    def swap(value):
        return lax.ppermute(value, "rep", [(0, 1), (1, 0)])

    ways = [-1, 1]

    def along(way, value, sources):
        return lax.ppermute(value, "amp", [(i, i + ways[way]) for i in sources])

    def packed(start, cuts):
        pos = jnp.stack([me, mine, jnp.asarray(start, jnp.int32)])
        return pos, pack(integrals, occ_irreps, virt_irreps, pos, groups, c_blk, tile, cuts)

    hops = chips - 1
    pos, (own,) = packed(0, [(0, OWN)])
    sister_own = swap(own)
    halves = split(pos, occ_irreps, virt_irreps, own, sister_own, k_local, c_local, c_blk, tile)

    occ = lax.dynamic_slice_in_dim(occ_irreps, me * k_local, k_local)
    block_labels = jnp.repeat(virt_irreps, tile // c_blk).reshape(parts, blocks)
    allowed = (occ[:, None, None] == block_labels.T[None]).reshape(entries, parts)
    ranks = jnp.cumsum(allowed.astype(jnp.int32), axis=0) - 1
    counts = ranks[-1] + 1

    def places(ident):
        ent, dev = ident // parts, ident % parts
        k_of = jnp.where(ident < 0, -1, ent // blocks)
        return k_of, jnp.where(ident < 0, 0, dev * c_local + (ent % blocks) * c_blk)

    def listed(where, count):
        hit = allowed[:, :, None] & (where[:, :, None] == jnp.arange(count, dtype=jnp.int32))
        ident = entry[:, None] * parts + device
        return jnp.sum(jnp.where(hit, ident[:, :, None] + 1, 0), axis=(0, 1)) - 1

    def across(value, shift):
        return lax.ppermute(value, "summa", [(i, (i + shift) % groups) for i in range(groups)])

    def gather_round(start):
        panel = lax.all_gather(packed(start, [(0, CAP)])[1][0], ("amp", "rep"))
        inside = (ranks >= start) & (ranks < start + CAP)
        k_of, off = places(listed(jnp.where(inside, ranks - start + device * CAP, -1), parts * CAP))
        received = []
        for phase in [*range(1, groups), 0]:
            views = [((d, phase), d * CAP, CAP, 0) for d in range(parts)]
            if phase:
                received.append(across(contract([panel] * parts, views, k_of, off, turned, c_blk)[0], phase))
        return contract([panel] * parts, views, k_of, off, turned, c_blk, received, inner)[0]

    every = (occ_irreps[:, None, None] == block_labels.T[None]).reshape(groups, entries, parts)
    every = jnp.sum(every.astype(jnp.int32), axis=1)
    in_chip = jnp.max(every.reshape(groups, chips, cores).sum(2))
    fits = (jnp.max(every) <= OWN) & (in_chip <= 2 * SHARE)
    own_verdict = jnp.stack([1 - fits.astype(jnp.int32), jnp.max(every)])
    verdict = own_verdict
    mols = lax.axis_size("mol")
    for shift in range(1, mols):
        turn = [(i, (i + shift) % mols) for i in range(mols)]
        verdict = jnp.maximum(verdict, lax.ppermute(own_verdict, "mol", turn))

    base_hops = 2 * OWN
    total = base_hops + 2 * hops * 2 * SHARE
    dz = device // cores - z
    way = (dz < 0).astype(jnp.int32)
    first_count = jnp.repeat(counts.reshape(chips, cores)[:, 0], cores)
    combined = ranks + jnp.where(device % cores == 1, first_count, 0)
    sister = (combined % 2 != core).astype(jnp.int32)
    at_hop = base_hops + ((way * hops + jnp.abs(dz) - 1) * 2 + sister) * SHARE + combined // 2
    where = jnp.where(dz == 0, jnp.where(device % cores == core, 0, OWN) + ranks, at_hop)
    k_of, off = places(listed(where, total))

    def sums(sources, **more):
        return contract([one[0] for one in sources], [one[1:] for one in sources], k_of, off, turned, c_blk, **more)

    order = [*range(1, groups), 0]
    moved = {phase: [None] for phase in order}
    swapped = {phase: [None] for phase in order}

    def send(phase, values):
        h = len(moved[phase])
        sources = [range(1, chips - h + 1), range(h - 1, chips - 1)]
        moved[phase].append([along(way, values[way], sources[way]) for way in range(2)])

    def from_hop(h, phase):
        out = []
        for way in range(2):
            start = base_hops + (way * hops + h - 1) * 2 * SHARE
            out.append((moved[phase][h][way], (), start, SHARE, 0))
            out.append((swapped[phase][h][way], (), start + SHARE, SHARE, 0))
        return out

    for phase in order:
        send(phase, [halves[phase]] * 2)
    near = [(own, (slice(None),), 0, OWN, 0), (sister_own, (slice(None),), OWN, OWN, 0)]
    near = sums(near, width=groups)
    part = {phase: [near[phase]] for phase in order}
    for h in range(1, hops):
        for phase in order:
            if h > 1:
                part[phase] = sums(from_hop(h - 1, phase), adds=part[phase])
            decided = [verdict] if h == hops - 1 and phase == order[-1] else []
            here = together(moved[phase][h], [*part[phase], *decided])
            moved[phase][h] = here
            swapped[phase].append([swap(one) for one in here])
            send(phase, here)
    received = []
    for phase in order:
        swapped[phase].append([swap(one) for one in moved[phase][hops]])
        if hops > 1:
            part[phase] = sums(from_hop(hops - 1, phase), adds=part[phase])
        last = sums(from_hop(hops, phase), adds=part[phase])
        if phase:
            received.append(across(last[0], phase))
    (first,) = sums([(own, (0,), 0, 0, 0)], adds=[*last, *received], final=inner)

    failed, most = verdict[0], verdict[1]

    def more(state):
        return state[0] < most

    def step(state):
        start, value = state
        return start + CAP, jnp.where(start == 0, 0.0, value) + gather_round(start)

    return lax.while_loop(more, step, (jnp.where(failed > 0, 0, most), first))[1]


def solution(mesh):
    return jax.shard_map(
        body,
        mesh=mesh,
        in_specs=(
            P(("mol", "summa"), ("amp", "rep"), None, None),
            P(("mol", "summa"), ("amp", "rep"), None, None),
            P("mol"),
            P("mol"),
        ),
        out_specs=P(("mol", "summa"), None, ("amp", "rep"), None),
        check_vma=False,
    )
```
